512 devices in a mesh: row: 16 (over z), col: 32 (over x, y, core).
Axes of the slice: x: 4, y: 4, z: 16, core: 2. Of those that a mesh axis runs over, the one named last changes fastest.
Arguments:
- features: bfloat16 [65536, 128], P(('row', 'col')), may hold values from -6 to 6
- weight: bfloat16 [128, 256], replicated, may hold values from -0.5 to 0.5
- bias: float32 [256], replicated, may hold values from -3 to 3
- adj_values: bfloat16 [16, 512, 6, 128, 128], P('row', 'col'), may hold values from -0.109375 to 0.109375
- adj_rows: int32 [16, 512, 6], P('row', 'col'), may hold values from -1 to 31, as said below
- cotangent: bfloat16 [65536, 256], P(('row', 'col')), may hold values from -6 to 6
Outputs:
- activations: bfloat16 [65536, 256], P(('row', 'col'))
- dfeatures: bfloat16 [65536, 128], P(('row', 'col'))
- dweight: float32 [128, 256], replicated
- dbias: float32 [256], replicated
The draws below stay inside these ranges and needn't reach their ends.
Inputs may be any that keep to these rules, and one draw needn't show every extreme that they name: `adj_rows`: in each block column of each tile the live slots come first and name distinct block rows, the rest are -1; every tile has some block column with all 6 slots live.
All inputs are finite; a program needn't handle non-finite values.
Results may differ from the reference program's by a relative error of at most 0.024.
Values may be sent and summed in bfloat16 or wider, within the bound.
A program may use at most 128 MiB of HBM per device.

```python
import jax
import jax.numpy as jnp
from jax import lax

F_IN = 128
F_OUT = 256
BLOCK = 128
ROWS_DEV = 128
SLOTS = 6
DEV_BLOCKS = 1
ROW_BLOCKS = 32
COL_BLOCKS = 16
ALL_BLOCKS = 512
NODES = 65536
N_ROW = 16
N_COL = 32


def draw_adj_rows(key, part):
    key = jax.random.fold_in(key, 7)
    key_score, key_near, key_far = jax.random.split(key, 3)
    dev_blocks = ROWS_DEV // BLOCK
    row_blocks = N_COL * dev_blocks
    col_blocks = N_ROW * dev_blocks
    all_blocks = N_COL * col_blocks
    column = jnp.arange(all_blocks, dtype=jnp.int32)
    tile_col = column // col_blocks
    within = column % col_blocks
    diag_tile = within // dev_blocks
    diagonal_block_local = tile_col * dev_blocks + within % dev_blocks
    tile_row = jnp.arange(N_ROW, dtype=jnp.int32)[:, None]
    distance = jnp.abs(tile_row - diag_tile[None, :])
    is_diagonal = distance == 0
    target_labels = jnp.arange(row_blocks, dtype=jnp.int32)
    block_scores = jax.random.randint(key_score, (N_ROW, all_blocks, row_blocks), 0, 1 << 16, dtype=jnp.int32) * row_blocks + target_labels
    extra_score = is_diagonal[:, :, None] & (target_labels[None, None, :] == diagonal_block_local[None, :, None])
    block_scores = block_scores + jnp.where(extra_score, 1 << 28, 0).astype(jnp.int32)
    chosen = lax.top_k(block_scores, SLOTS)[1].astype(jnp.int32)
    near_counts = jax.random.randint(key_near, (N_ROW, all_blocks), 1, SLOTS + 1, dtype=jnp.int32)
    far_counts = jax.random.randint(key_far, (N_ROW, all_blocks), 0, 2, dtype=jnp.int32)
    counts = jnp.where(is_diagonal, SLOTS, jnp.where(distance == 1, near_counts, far_counts))
    slot_index = jnp.arange(SLOTS, dtype=jnp.int32)
    return jnp.where(slot_index[None, None, :] < counts[:, :, None], chosen, -1).astype(jnp.int32)


def block_scale(stream_key, extent, pieces, least, top_value):
    loudness = 1.0
    for position, parts in pieces:
        draws = jax.random.uniform(jax.random.fold_in(jax.random.fold_in(stream_key, 6), position), (parts,), jnp.float32, least / len(pieces), top_value / len(pieces))
        loudness = loudness * jnp.repeat(jnp.exp(draws), extent[position] // parts).reshape((-1,) + (1,) * (len(extent) - 1 - position))
    return loudness


def gaussian(stream_key, dims, scale, most, cuts=(), kind=jnp.bfloat16):
    result = jax.random.normal(stream_key, dims, jnp.float32) * scale
    if len(cuts) > 0:
        result = block_scale(stream_key, dims, cuts, -0.22, 0.18) * result
    return jnp.clip(result, min=-most, max=most).astype(kind)


def setup_inputs(seed: int = 0) -> dict:
    splits = jax.random.split(jax.random.key(seed), 7)
    features = gaussian(splits[0], (NODES, F_IN), 1.0, 6.0, ((0, 512),))
    weight = gaussian(splits[1], (F_IN, F_OUT), F_IN ** -0.5, 0.5)
    bias = gaussian(splits[2], (F_OUT,), 0.5, 3.0, (), jnp.float32)
    adj_values = gaussian(splits[3], (N_ROW, ALL_BLOCKS, SLOTS, BLOCK, BLOCK), (BLOCK * SLOTS * 4) ** -0.5, 0.109375, ((0, 16), (1, 32)))
    adj_rows = draw_adj_rows(jax.random.fold_in(splits[6], 71), 0)
    cotangent = gaussian(splits[5], (NODES, F_OUT), 1.0, 6.0, ((0, 512),))
    return {"features": features, "weight": weight, "bias": bias, "adj_values": adj_values, "adj_rows": adj_rows, "cotangent": cotangent}


def column_order(matrix):
    width = matrix.shape[-1]
    reshaped = matrix.reshape(N_ROW, N_COL, DEV_BLOCKS, BLOCK, width)
    return jnp.transpose(reshaped, (1, 0, 2, 3, 4)).reshape(N_COL, COL_BLOCKS, BLOCK, width)


def node_order(stacked):
    width = stacked.shape[-1]
    reshaped = stacked.reshape(N_COL, N_ROW, DEV_BLOCKS, BLOCK, width)
    return jnp.transpose(reshaped, (1, 0, 2, 3, 4)).reshape(NODES, width)


def selector(row_ids):
    target_labels = jnp.arange(ROW_BLOCKS, dtype=jnp.int32)
    return (row_ids.reshape(1, -1) == target_labels[:, None]).astype(jnp.float32)


def tile_forward(blocks, row_ids, column_list):
    contrib = jnp.einsum("tsij,tjf->tsif", blocks.astype(jnp.float32), column_list, precision=lax.Precision.HIGHEST)
    contrib = contrib.reshape(COL_BLOCKS * SLOTS, BLOCK * F_OUT)
    summed = jnp.dot(selector(row_ids), contrib, precision=lax.Precision.HIGHEST)
    return summed.reshape(ROW_BLOCKS * BLOCK, F_OUT).astype(jnp.bfloat16)


def tile_backward(blocks, row_ids, grads):
    flat = grads.reshape(ROW_BLOCKS, BLOCK * F_OUT).astype(jnp.float32)
    picked = jnp.dot(selector(row_ids).T, flat, precision=lax.Precision.HIGHEST)
    picked = picked.reshape(COL_BLOCKS, SLOTS, BLOCK, F_OUT)
    contrib = jnp.einsum("tsij,tsif->tjf", blocks.astype(jnp.float32), picked, precision=lax.Precision.HIGHEST)
    return contrib.astype(jnp.bfloat16)


def reference(features, weight, bias, adj_values, adj_rows, cotangent):
    transformed = jnp.dot(features, weight, preferred_element_type=jnp.float32).astype(jnp.bfloat16)
    column_list = column_order(transformed).astype(jnp.float32)
    blocks_all = adj_values.reshape(N_ROW, N_COL, COL_BLOCKS, SLOTS, BLOCK, BLOCK)
    ids_all = adj_rows.reshape(N_ROW, N_COL, COL_BLOCKS, SLOTS)

    def row_forward_pass(row_index):
        def add_tile(total, col_index):
            tile = tile_forward(blocks_all[row_index, col_index], ids_all[row_index, col_index], column_list[col_index])
            return total + tile.astype(jnp.float32), None

        start_sum = jnp.zeros((ROW_BLOCKS * BLOCK, F_OUT), jnp.float32)
        total, unused = lax.scan(add_tile, start_sum, jnp.arange(N_COL))
        return total

    hidden = lax.map(row_forward_pass, jnp.arange(N_ROW)).reshape(NODES, F_OUT)
    preact = hidden + bias[None, :]
    gate = jax.nn.sigmoid(preact)
    activations = (preact * gate).astype(jnp.bfloat16)
    dpre = cotangent.astype(jnp.float32) * gate * (1.0 + preact * (1.0 - gate))
    dbias = jnp.sum(dpre, axis=0)
    grads_rows = dpre.astype(jnp.bfloat16).reshape(N_ROW, ROW_BLOCKS * BLOCK, F_OUT)

    def backward_row(total, row_index):
        def one_tile(col_index):
            return tile_backward(blocks_all[row_index, col_index], ids_all[row_index, col_index], grads_rows[row_index])

        tiles = lax.map(one_tile, jnp.arange(N_COL))
        return total + tiles.astype(jnp.float32), None

    start_grad = jnp.zeros((N_COL, COL_BLOCKS, BLOCK, F_OUT), jnp.float32)
    dcolumns, unused = lax.scan(backward_row, start_grad, jnp.arange(N_ROW))
    dtransformed = node_order(dcolumns).astype(jnp.bfloat16)
    dfeatures = jnp.dot(dtransformed, weight.T, preferred_element_type=jnp.float32).astype(jnp.bfloat16)
    dweight = jnp.dot(features.T, dtransformed, preferred_element_type=jnp.float32)
    return activations, dfeatures, dweight, dbias
```

```python
import jax
import jax.numpy as jnp
from jax import lax
from jax.experimental import pallas as pl
from jax.experimental.pallas import tpu as pltpu
from jax.sharding import PartitionSpec as P

MESH = pl.DeviceIdType.MESH
BF16 = jnp.bfloat16
F32 = jnp.float32
BLOCK = 128
F_IN = 128
F_OUT = 256
SLOTS = 6
NZ = 16
SIDE = 4
CHIPS = SIDE * SIDE
NCOL = 2 * CHIPS
DEAD = NZ * SLOTS
FAR_FIRST = (8, 7, -7, -6, 6, 5, -5, -4, 4, 3, -3, -2, 2, 1, -1)


def remote(src, dst, send_sem, recv_sem, device):
    return pltpu.make_async_remote_copy(
        src_ref=src,
        dst_ref=dst,
        send_sem=send_sem,
        recv_sem=recv_sem,
        device_id=device,
        device_id_type=MESH,
    )


def toward(b):
    if abs(b) <= 2:
        return 0
    return b - 2 if b > 0 else b + 2


def behind(b):
    far = b + 2 if b > 0 else b - 2
    return far if far in FAR_FIRST else None


def kernel(
    adj, feat, weight, bias, vals, cot,
    act_out, df_out, dw_out, db_out,
    xa, blk, prod, inv, w_v, b_v, c_v, act_v,
    sd, rd, sz, rz, ga, own, sb, rb, df_v,
    dwp, dwr, dwm, dwx, dwz, dwf, dwo, dbo,
    lsem, zs, zr, ds, dr, xs, xr, gs, gr, fs, fr, bs, br, ws, wr,
    wxs, wxr, wzs, wzr, was, war,
):
    z = lax.axis_index("row")
    c = lax.axis_index("col")
    px, py, core = c // 8, (c // 2) % 4, c % 2
    other = 1 - core

    def ring(off):
        return lax.rem(z + (off + 2 * NZ), NZ)

    def at_z(off):
        return (ring(off), c)

    def chip(i, sign):
        j = lax.rem(i + 1, CHIPS)
        dx, dy = j // SIDE, lax.rem(j, SIDE)
        qx = lax.rem(px + SIDE + sign * dx, SIDE)
        qy = lax.rem(py + SIDE + sign * dy, SIDE)
        return qx * SIDE + qy

    def at_chip(i):
        return (z, 2 * chip(i, 1) + core)

    twin = (z, 2 * (px * SIDE + py) + other)

    ld_x = pltpu.make_async_copy(feat, xa.at[z], lsem.at[0])
    ld_a = pltpu.make_async_copy(vals, blk, lsem.at[1])
    ld_w = pltpu.make_async_copy(weight, w_v, lsem.at[2])
    ld_b = pltpu.make_async_copy(bias, b_v, lsem.at[3])
    ld_c = pltpu.make_async_copy(cot, c_v, lsem.at[4])
    for ld in (ld_x, ld_a, ld_w, ld_b, ld_c):
        ld.start()

    barrier = pltpu.get_barrier_semaphore()
    for off in (1, -1, 2, -2):
        pl.semaphore_signal(barrier, inc=1, device_id=at_z(off), device_id_type=MESH)
    pl.semaphore_signal(barrier, inc=1, device_id=twin, device_id_type=MESH)

    def greet(i, carry):
        pl.semaphore_signal(barrier, inc=1, device_id=at_chip(i), device_id_type=MESH)
        return carry

    lax.fori_loop(0, CHIPS - 1, greet, 0)

    prod[DEAD] = jnp.zeros((BLOCK, F_IN), F32)
    ga[NCOL] = jnp.zeros((F_IN, BLOCK), BF16)
    ld_x.wait()
    pl.semaphore_wait(barrier, 4 + 1 + CHIPS - 1)

    def invert(t, carry):
        ids = [adj[t, s] for s in range(SLOTS)]
        for k in range(NCOL):
            slot = jnp.int32(DEAD)
            for s in range(SLOTS):
                slot = jnp.where(ids[s] == k, t * SLOTS + s, slot)
            inv[t, k] = slot
        return carry

    def multiply(t):
        tall = blk[pl.ds(t * SLOTS, SLOTS)].reshape(SLOTS * BLOCK, BLOCK)
        out = jnp.dot(tall, xa[t], preferred_element_type=F32)
        prod[pl.ds(t * SLOTS, SLOTS)] = out.reshape(SLOTS, BLOCK, F_IN)

    sent = []
    arriving = {}
    for phase in range(4):
        for dist in (2 * phase + 1, 2 * phase + 2):
            for d in (1, -1):
                if dist == 8 and d == -1:
                    continue
                if phase == 0:
                    src, jump = ring(0), d * dist
                else:
                    arriving[d * (dist - 2)].wait_recv()
                    src, jump = ring(-d * (dist - 2)), 2 * d
                m = FAR_FIRST.index(d * dist)
                cp = remote(xa.at[src], xa.at[src], zs.at[m], zr.at[m], at_z(jump))
                cp.start()
                sent.append(cp)
                arriving[d * dist] = cp
        lax.fori_loop(4 * phase, 4 * phase + 4, invert, 0)
        if phase == 0:
            ld_a.wait()
            multiply(z)
        else:

            def multiply_pair(i, carry):
                dist = 2 * phase - 1 + i // 2
                multiply(ring((2 * lax.rem(i, 2) - 1) * dist))
                return carry

            lax.fori_loop(0, 4 if phase < 3 else 3, multiply_pair, 0)
    for off in (7, -7, -6, 8):
        arriving[off].wait_recv()
        multiply(ring(-off))

    def placed(k):
        total = prod[inv[0, k]]
        for t in range(1, NZ):
            total = total + prod[inv[t, k]]
        return total

    def to_twin(i, carry):
        sd[i] = placed(2 * chip(i, 1) + other).astype(BF16)
        remote(sd.at[i], rd.at[i], ds.at[i], dr.at[i], twin).start()
        return carry

    lax.fori_loop(0, CHIPS, to_twin, 0)

    def both(i):
        mine = placed(2 * chip(i, 1) + core)
        remote(sd.at[i], rd.at[i], ds.at[i], dr.at[i], twin).wait_recv()
        return mine + rd[i].astype(F32)

    def to_owner(i, carry):
        sz[i] = both(i).astype(BF16)
        remote(sz.at[i], rz.at[i], xs.at[i], xr.at[i], at_chip(i)).start()
        return carry

    lax.fori_loop(0, CHIPS - 1, to_owner, 0)
    own[0] = both(CHIPS - 1)

    def collect(i, carry):
        remote(sz.at[i], rz.at[i], xs.at[i], xr.at[i], at_chip(i)).wait_recv()
        own[0] += rz[i].astype(F32)
        return carry

    lax.fori_loop(0, CHIPS - 1, collect, 0)

    ld_w.wait()
    ld_b.wait()
    ld_c.wait()
    agg = own[0]
    agg_hi = agg.astype(BF16)
    agg_lo = (agg - agg_hi.astype(F32)).astype(BF16)
    w = w_v[...]
    hidden = jnp.dot(agg_hi, w, preferred_element_type=F32)
    hidden = hidden + jnp.dot(agg_lo, w, preferred_element_type=F32)
    preact = hidden + b_v[...]
    gate = jax.nn.sigmoid(preact)
    act_v[...] = (preact * gate).astype(BF16)
    st_act = pltpu.make_async_copy(act_v, act_out, lsem.at[5])
    st_act.start()
    dpre = c_v[...].astype(F32) * gate * (1.0 + preact * (1.0 - gate))
    dpre_round = dpre.astype(BF16)
    ga[c] = lax.dot_general(
        w, dpre_round, (((1,), (1,)), ((), ())), preferred_element_type=F32
    ).astype(BF16)

    def spread(i, carry):
        remote(ga.at[c], ga.at[c], gs.at[i], gr.at[i], at_chip(i)).start()
        return carry

    lax.fori_loop(0, CHIPS - 1, spread, 0)
    g_twin = remote(ga.at[c], ga.at[c], gs.at[CHIPS - 1], gr.at[CHIPS - 1], twin)
    g_twin.start()

    tn = (((0,), (0,)), ((), ()))
    dw = lax.dot_general(agg_hi, dpre_round, tn, preferred_element_type=F32)
    dw = dw + lax.dot_general(agg_lo, dpre_round, tn, preferred_element_type=F32)
    db = jnp.sum(dpre, axis=0, keepdims=True)
    first = lax.broadcasted_iota(jnp.int32, (8, F_OUT), 0) == 0
    db8 = jnp.where(first, jnp.broadcast_to(db, (8, F_OUT)), 0.0)
    for half in range(2):
        lanes = slice(half * 128, half * 128 + 128)
        dwp[half, 0:F_IN] = dw[:, lanes]
        dwp[half, F_IN : F_IN + 8] = db8[:, lanes]
    w_twin = remote(dwp.at[other], dwr, ws.at[0], wr.at[0], twin)
    w_twin.start()
    w_twin.wait_recv()
    for p in range(CHIPS):
        dwm[p, 0:8] = dwp[core, 8 * p : 8 * p + 8] + dwr[8 * p : 8 * p + 8]
    db_half = dwp[core, F_IN : F_IN + 8] + dwr[F_IN : F_IN + 8]
    for p in range(CHIPS):
        dwm[p, 8:16] = db_half

    def w_spread(i, carry):
        remote(dwm.at[chip(i, 1)], dwx.at[i], wxs.at[i], wxr.at[i], at_chip(i)).start()
        return carry

    lax.fori_loop(0, CHIPS - 1, w_spread, 0)

    def forward(i, carry):
        src = 2 * chip(i, -1) + core
        remote(ga.at[src], ga.at[src], gs.at[i], gr.at[i], at_chip(i)).wait_recv()
        remote(ga.at[src], ga.at[src], fs.at[i], fr.at[i], twin).start()
        return carry

    lax.fori_loop(0, CHIPS - 1, forward, 0)

    dwz[z] = dwm[px * SIDE + py]

    def w_collect(i, carry):
        remote(dwm.at[0], dwx.at[i], wxs.at[i], wxr.at[i], at_chip(i)).wait_recv()
        dwz[z] += dwx[i]
        return carry

    lax.fori_loop(0, CHIPS - 1, w_collect, 0)

    def w_ring(i):
        return remote(dwz.at[z], dwz.at[z], wzs.at[i], wzr.at[i], at_z(i + 1))

    def w_ring_start(i, carry):
        w_ring(i).start()
        return carry

    lax.fori_loop(0, NZ - 1, w_ring_start, 0)

    g_twin.wait_recv()

    def from_twin(i, carry):
        src = 2 * chip(i, -1) + other
        remote(ga.at[src], ga.at[src], fs.at[i], fr.at[i], twin).wait_recv()
        return carry

    lax.fori_loop(0, CHIPS - 1, from_twin, 0)

    def pull(i, carry):
        q, r = i // 4, lax.rem(i, 4)
        t = ring(-jnp.where(r < 2, 8 - 2 * q - r, 7 + 2 * q + r))
        picks = []
        for s in range(SLOTS):
            k = adj[t, s]
            picks.append(ga[jnp.where(k < 0, NCOL, k)])
        wide = jnp.concatenate(picks, axis=1)
        tall = blk[pl.ds(t * SLOTS, SLOTS)].reshape(SLOTS * BLOCK, BLOCK)
        own[i] = jnp.dot(wide, tall, preferred_element_type=F32)
        return carry

    def b_copy(m):
        b = FAR_FIRST[m]
        return remote(sb.at[m], rb.at[m], bs.at[m], br.at[m], at_z(toward(b) - b))

    def reduce_group(phase):
        for m in range(4 * phase, min(4 * phase + 4, NZ - 1)):
            far = behind(FAR_FIRST[m])
            if far is None:
                sb[m] = own[m].astype(BF16)
            else:
                n = FAR_FIRST.index(far)
                b_copy(n).wait_recv()
                sb[m] = (own[m] + rb[n].astype(F32)).astype(BF16)
            b_copy(m).start()

    lax.fori_loop(0, 4, pull, 0)
    reduce_group(0)
    lax.fori_loop(4, 16, pull, 0)
    reduce_group(1)
    reduce_group(2)

    def w_sum(i, total):
        w_ring(i).wait_recv()
        return total

    lax.fori_loop(0, NZ - 1, w_sum, 0)
    piece = dwz[0]
    for t in range(1, NZ):
        piece = piece + dwz[t]
    me = px * SIDE + py
    dwf[core, CHIPS] = piece[8:16]
    dwf[core, me] = piece[0:8]

    def w_gather(i, src):
        return remote(
            dwf.at[core, src], dwf.at[core, src], was.at[i], war.at[i], at_chip(i)
        )

    def w_gather_start(i, carry):
        w_gather(i, me).start()
        return carry

    lax.fori_loop(0, CHIPS - 1, w_gather_start, 0)

    reduce_group(3)

    def w_gather_wait(i, carry):
        w_gather(i, chip(i, -1)).wait_recv()
        return carry

    lax.fori_loop(0, CHIPS - 1, w_gather_wait, 0)
    w_back = remote(dwf.at[core], dwf.at[core], ws.at[1], wr.at[1], twin)
    w_back.start()

    total = own[NZ - 1]
    for b in (2, 1, -1, -2):
        n = FAR_FIRST.index(b)
        b_copy(n).wait_recv()
        total = total + rb[n].astype(F32)
    df_v[...] = total.T.astype(BF16)
    st_df = pltpu.make_async_copy(df_v, df_out, lsem.at[6])
    st_df.start()

    w_in = remote(dwf.at[other], dwf.at[other], ws.at[1], wr.at[1], twin)
    w_in.wait_recv()
    for half in range(2):
        lanes = slice(half * 128, half * 128 + 128)
        dwo[:, lanes] = dwf[half, 0:CHIPS].reshape(F_IN, 128)
        dbo[:, lanes] = dwf[half, CHIPS, 0:1]
    st_dw = pltpu.make_async_copy(dwo, dw_out, lsem.at[7])
    st_dw.start()
    st_db = pltpu.make_async_copy(dbo, db_out, lsem.at[8])
    st_db.start()

    for cp in sent:
        cp.wait_send()

    def drain(i, carry):
        remote(sd.at[i], rd.at[i], ds.at[i], dr.at[i], twin).wait_send()
        remote(ga.at[c], ga.at[c], gs.at[i], gr.at[i], twin).wait_send()
        return carry

    lax.fori_loop(0, CHIPS, drain, 0)

    def drain_15(i, carry):
        remote(sz.at[i], rz.at[i], xs.at[i], xr.at[i], twin).wait_send()
        remote(ga.at[c], ga.at[c], fs.at[i], fr.at[i], twin).wait_send()
        remote(dwm.at[0], dwx.at[i], wxs.at[i], wxr.at[i], twin).wait_send()
        remote(dwz.at[z], dwz.at[z], wzs.at[i], wzr.at[i], twin).wait_send()
        w_gather(i, me).wait_send()
        remote(sb.at[i], rb.at[i], bs.at[i], br.at[i], twin).wait_send()
        return carry

    lax.fori_loop(0, CHIPS - 1, drain_15, 0)
    w_twin.wait_send()
    w_back.wait_send()
    for st in (st_act, st_df, st_dw, st_db):
        st.wait()


def local(features, weight, bias, adj_values, adj_rows, cotangent):
    any_space = pl.BlockSpec(memory_space=pl.ANY)
    dma = pltpu.SemaphoreType.DMA
    outs = pl.pallas_call(
        kernel,
        out_shape=(
            jax.ShapeDtypeStruct((BLOCK, F_OUT), BF16),
            jax.ShapeDtypeStruct((BLOCK, F_IN), BF16),
            jax.ShapeDtypeStruct((F_IN, F_OUT), F32),
            jax.ShapeDtypeStruct((1, F_OUT), F32),
        ),
        in_specs=[pl.BlockSpec(memory_space=pltpu.SMEM)] + [any_space] * 5,
        out_specs=[any_space] * 4,
        scratch_shapes=[
            pltpu.VMEM((NZ, BLOCK, F_IN), BF16),
            pltpu.VMEM((DEAD, BLOCK, BLOCK), BF16),
            pltpu.VMEM((DEAD + 1, BLOCK, F_IN), F32),
            pltpu.SMEM((NZ, NCOL), jnp.int32),
            pltpu.VMEM((F_IN, F_OUT), BF16),
            pltpu.VMEM((1, F_OUT), F32),
            pltpu.VMEM((BLOCK, F_OUT), BF16),
            pltpu.VMEM((BLOCK, F_OUT), BF16),
            pltpu.VMEM((CHIPS, BLOCK, F_IN), BF16),
            pltpu.VMEM((CHIPS, BLOCK, F_IN), BF16),
            pltpu.VMEM((CHIPS - 1, BLOCK, F_IN), BF16),
            pltpu.VMEM((CHIPS - 1, BLOCK, F_IN), BF16),
            pltpu.VMEM((NCOL + 1, F_IN, BLOCK), BF16),
            pltpu.VMEM((NZ, F_IN, BLOCK), F32),
            pltpu.VMEM((NZ - 1, F_IN, BLOCK), BF16),
            pltpu.VMEM((NZ - 1, F_IN, BLOCK), BF16),
            pltpu.VMEM((BLOCK, F_IN), BF16),
            pltpu.VMEM((2, F_IN + 8, 128), F32),
            pltpu.VMEM((F_IN + 8, 128), F32),
            pltpu.VMEM((CHIPS, 16, 128), F32),
            pltpu.VMEM((CHIPS - 1, 16, 128), F32),
            pltpu.VMEM((NZ, 16, 128), F32),
            pltpu.VMEM((2, CHIPS + 1, 8, 128), F32),
            pltpu.VMEM((F_IN, F_OUT), F32),
            pltpu.VMEM((1, F_OUT), F32),
            dma((9,)),
            dma((15,)), dma((15,)),
            dma((16,)), dma((16,)),
            dma((15,)), dma((15,)),
            dma((16,)), dma((16,)),
            dma((15,)), dma((15,)),
            dma((15,)), dma((15,)),
            dma((2,)), dma((2,)),
            dma((15,)), dma((15,)),
            dma((15,)), dma((15,)),
            dma((15,)), dma((15,)),
        ],
        compiler_params=pltpu.CompilerParams(
            collective_id=0, has_side_effects=True, vmem_limit_bytes=56 << 20
        ),
    )(
        adj_rows[0],
        features,
        weight,
        bias.reshape(1, F_OUT),
        adj_values.reshape(DEAD, BLOCK, BLOCK),
        cotangent,
    )
    activations, dfeatures, dweight, dbias = outs
    return activations, dfeatures, dweight, dbias.reshape(F_OUT)


def solution(mesh):
    return jax.shard_map(
        local,
        mesh=mesh,
        in_specs=(
            P(("row", "col"), None),
            P(),
            P(),
            P("row", "col", None, None, None),
            P("row", "col", None),
            P(("row", "col"), None),
        ),
        out_specs=(P(("row", "col"), None), P(("row", "col"), None), P(), P()),
        check_vma=False,
    )
```

```python
import jax
import jax.numpy as jnp
from jax import lax
from jax.experimental import pallas as pl
from jax.experimental.pallas import tpu as pltpu
from jax.sharding import PartitionSpec as P

MESH = pl.DeviceIdType.MESH
BF16 = jnp.bfloat16
F32 = jnp.float32
BLOCK = 128
F_IN = 128
F_OUT = 256
SLOTS = 6
NZ = 16
SIDE = 4
CHIPS = SIDE * SIDE
NCOL = 2 * CHIPS
DEAD = NZ * SLOTS
LAG = 5
HALFWAY = 0
GATHER = (
    ((0, 3), (0, -3), (0, 1), (0, -1)),
    ((3, 6), (-3, -6), (1, 2), (-1, -2), (3, 4), (-3, -4)),
    ((6, 8), (6, 7), (-6, -7), (6, 5), (-6, -5)),
)
REDUCE = (
    ((8, 6), (7, 6), (-7, -6), (5, 6), (-5, -6), (4, 3), (-4, -3), (1, 0), (-1, 0)),
    ((6, 3), (-6, -3), (2, 0), (-2, 0)),
    ((3, 0), (-3, 0)),
)


def remote(src, dst, send_sem, recv_sem, device):
    return pltpu.make_async_remote_copy(
        src_ref=src,
        dst_ref=dst,
        send_sem=send_sem,
        recv_sem=recv_sem,
        device_id=device,
        device_id_type=MESH,
    )


def kernel(
    adj, feat, weight, bias, vals, cot,
    act_out, df_out, dw_out, db_out,
    xa, blk, prod, inv, w_v, b_v, c_v, act_v,
    sd, rd, sz, rz, ga, own, sb, rb, df_v,
    dwm, dwx, dwt, dwz, dwf, dwo, dbo,
    lsem, asem, zs, zr, ds, dr, xs, xr, gs, gr, fs, fr, bs, br, ws, wr,
    wxs, wxr, wzs, wzr, was, war,
):
    z = lax.axis_index("row")
    c = lax.axis_index("col")
    px, py, core = c // 8, (c // 2) % 4, c % 2
    other = 1 - core

    def ring(off):
        return lax.rem(z + (off + 2 * NZ), NZ)

    def at_z(off):
        return (ring(off), c)

    def far_first(a):
        return jnp.where(a == 0, 2, jnp.where(a == 1, 1, jnp.where(a == 2, 3, 0)))

    def chip(i, sign):
        dx, dy = far_first(i // SIDE), far_first(lax.rem(i, SIDE))
        qx = lax.rem(px + SIDE + sign * dx, SIDE)
        qy = lax.rem(py + SIDE + sign * dy, SIDE)
        return qx * SIDE + qy

    def at_chip(i):
        return (z, 2 * chip(i, 1) + core)

    twin = (z, 2 * (px * SIDE + py) + other)

    ld_x = pltpu.make_async_copy(feat, xa.at[z], lsem.at[0])
    ld_w = pltpu.make_async_copy(weight, w_v, lsem.at[2])
    ld_b = pltpu.make_async_copy(bias, b_v, lsem.at[3])
    ld_c = pltpu.make_async_copy(cot, c_v, lsem.at[4])

    def ld_a(t):
        part = pl.ds(t * SLOTS, SLOTS)
        return pltpu.make_async_copy(vals.at[part], blk.at[part], asem.at[t])

    def ld_a_start(t, carry):
        ld_a(t).start()
        return carry

    barrier = pltpu.get_barrier_semaphore()
    for off in (3, -3, 1, -1):
        pl.semaphore_signal(barrier, inc=1, device_id=at_z(off), device_id_type=MESH)
    ld_x.start()

    def greet(i, carry):
        pl.semaphore_signal(barrier, inc=1, device_id=at_chip(i), device_id_type=MESH)
        return carry

    lax.fori_loop(0, CHIPS - 1, greet, 0)
    pl.semaphore_signal(barrier, inc=1, device_id=twin, device_id_type=MESH)

    prod[DEAD] = jnp.zeros((BLOCK, F_IN), F32)
    ga[NCOL] = jnp.zeros((F_IN, BLOCK), BF16)
    ld_x.wait()
    pl.semaphore_wait(barrier, 4 + 1 + CHIPS - 1)

    def invert(t, carry):
        ids = [adj[s, 0, t] for s in range(SLOTS)]
        for k in range(NCOL):
            slot = jnp.int32(DEAD)
            for s in range(SLOTS):
                slot = jnp.where(ids[s] == k, t * SLOTS + s, slot)
            inv[t, k] = slot
        return carry

    def multiply(t):
        ld_a(t).wait()
        tall = blk[pl.ds(t * SLOTS, SLOTS)].reshape(SLOTS * BLOCK, BLOCK)
        out = jnp.dot(tall, xa[t], preferred_element_type=F32)
        prod[pl.ds(t * SLOTS, SLOTS)] = out.reshape(SLOTS, BLOCK, F_IN)

    def hop(a, b):
        block = xa.at[ring(-a)]
        return remote(block, block, zs.at[b % NZ], zr.at[b % NZ], at_z(b - a))

    here = {0}

    def arrive(b):
        if b not in here:
            hop(0, b).wait_recv()
            here.add(b)

    for stage, edges in enumerate(GATHER):
        for a, b in edges:
            arrive(a)
            hop(a, b).start()
        if stage == 0:
            lax.fori_loop(0, NZ, ld_a_start, 0)
            for ld in (ld_w, ld_b, ld_c):
                ld.start()
        if stage < 2:
            lax.fori_loop(8 * stage, 8 * stage + 8, invert, 0)
        if stage == 1:
            for b in (0, 1, -1, 3, -3):
                multiply(ring(-b))
        if stage == 2:
            for b in (6, -6, 2, -2, 4, -4, 5, -5, 7, -7, 8):
                arrive(b)
                multiply(ring(-b))

    def placed(k):
        total = prod[inv[0, k]]
        for t in range(1, NZ):
            total = total + prod[inv[t, k]]
        return total

    def to_twin(i, carry):
        sd[i] = placed(2 * chip(i, 1) + other).astype(BF16)
        remote(sd.at[i], rd.at[i], ds.at[i], dr.at[i], twin).start()
        return carry

    def both(i):
        mine = placed(2 * chip(i, 1) + core)
        remote(sd.at[i], rd.at[i], ds.at[i], dr.at[i], twin).wait_recv()
        return mine + rd[i].astype(F32)

    def to_owner(i, carry):
        sz[i] = both(i).astype(BF16)
        remote(sz.at[i], rz.at[i], xs.at[i], xr.at[i], at_chip(i)).start()
        return carry

    def to_both(i, carry):
        to_twin(i, carry)
        return to_owner(i - LAG, carry)

    lax.fori_loop(0, LAG, to_twin, 0)
    lax.fori_loop(LAG, CHIPS, to_both, 0)
    lax.fori_loop(CHIPS - LAG, CHIPS - 1, to_owner, 0)
    own[0] = both(CHIPS - 1)

    def collect(i, carry):
        remote(sz.at[i], rz.at[i], xs.at[i], xr.at[i], at_chip(i)).wait_recv()
        own[0] += rz[i].astype(F32)
        return carry

    lax.fori_loop(0, CHIPS - 1, collect, 0)

    ld_w.wait()
    ld_b.wait()
    ld_c.wait()
    agg = own[0]
    agg_hi = agg.astype(BF16)
    agg_lo = (agg - agg_hi.astype(F32)).astype(BF16)
    w = w_v[...]
    hidden = jnp.dot(agg_hi, w, preferred_element_type=F32)
    hidden = hidden + jnp.dot(agg_lo, w, preferred_element_type=F32)
    preact = hidden + b_v[...]
    gate = jax.nn.sigmoid(preact)
    act_v[...] = (preact * gate).astype(BF16)
    st_act = pltpu.make_async_copy(act_v, act_out, lsem.at[5])
    st_act.start()
    dpre = c_v[...].astype(F32) * gate * (1.0 + preact * (1.0 - gate))
    dpre_round = dpre.astype(BF16)
    ga[c] = lax.dot_general(
        w, dpre_round, (((1,), (1,)), ((), ())), preferred_element_type=F32
    ).astype(BF16)

    tn = (((0,), (0,)), ((), ()))
    dw = lax.dot_general(agg_hi, dpre_round, tn, preferred_element_type=F32)
    dw = dw + lax.dot_general(agg_lo, dpre_round, tn, preferred_element_type=F32)
    db = jnp.sum(dpre, axis=0, keepdims=True)
    first = lax.broadcasted_iota(jnp.int32, (8, F_OUT), 0) == 0
    db8 = jnp.where(first, jnp.broadcast_to(db, (8, F_OUT)), 0.0)
    for p in range(CHIPS):
        both_parts = jnp.concatenate([dw[8 * p : 8 * p + 8], db8], axis=0)
        dwm[p] = both_parts.astype(BF16)

    def w_spread(i, carry):
        remote(dwm.at[chip(i, 1)], dwx.at[i], wxs.at[i], wxr.at[i], at_chip(i)).start()
        return carry

    lax.fori_loop(0, CHIPS - 1, w_spread, 0)

    def spread(i, carry):
        remote(ga.at[c], ga.at[c], gs.at[i], gr.at[i], at_chip(i)).start()
        return carry

    lax.fori_loop(0, CHIPS - 1, spread, 0)
    g_twin = remote(ga.at[c], ga.at[c], gs.at[CHIPS - 1], gr.at[CHIPS - 1], twin)
    g_twin.start()

    def w_collect(i, total):
        remote(dwm.at[0], dwx.at[i], wxs.at[i], wxr.at[i], at_chip(i)).wait_recv()
        return total + dwx[i].astype(F32)

    me = px * SIDE + py
    mixed = lax.fori_loop(0, CHIPS - 1, w_collect, dwm[me].astype(F32))
    left, right = mixed[:, 0:128], mixed[:, 128:F_OUT]
    dwt[0] = jnp.where(core == 0, right, left)
    w_twin = remote(dwt.at[0], dwt.at[1], ws.at[0], wr.at[0], twin)
    w_twin.start()

    def forward(i, carry):
        src = 2 * chip(i, -1) + core
        remote(ga.at[src], ga.at[src], gs.at[i], gr.at[i], at_chip(i)).wait_recv()
        remote(ga.at[src], ga.at[src], fs.at[i], fr.at[i], twin).start()
        return carry

    lax.fori_loop(0, HALFWAY, forward, 0)
    w_twin.wait_recv()
    dwz[z] = (jnp.where(core == 0, left, right) + dwt[1]).astype(BF16)

    def w_ring(i):
        return remote(dwz.at[z], dwz.at[z], wzs.at[i], wzr.at[i], at_z(i + 1))

    def w_ring_start(i, carry):
        w_ring(i).start()
        return carry

    lax.fori_loop(0, NZ - 1, w_ring_start, 0)
    lax.fori_loop(HALFWAY, CHIPS - 1, forward, 0)

    g_twin.wait_recv()

    def from_twin(i, carry):
        src = 2 * chip(i, -1) + other
        remote(ga.at[src], ga.at[src], fs.at[i], fr.at[i], twin).wait_recv()
        return carry

    lax.fori_loop(0, CHIPS - 1, from_twin, 0)

    def pull(i, carry):
        t = ring(-i)
        picks = []
        for s in range(SLOTS):
            k = adj[s, 0, t]
            picks.append(ga[jnp.where(k < 0, NCOL, k)])
        wide = jnp.concatenate(picks, axis=1)
        tall = blk[pl.ds(t * SLOTS, SLOTS)].reshape(SLOTS * BLOCK, BLOCK)
        own[i] = jnp.dot(wide, tall, preferred_element_type=F32)
        return carry

    def back(a, b):
        n = a % NZ
        return remote(sb.at[n], rb.at[n], bs.at[n], br.at[n], at_z(b - a))

    def summed(b):
        total = own[b % NZ]
        for edges in REDUCE:
            for a, to in edges:
                if to == b:
                    back(a, b).wait_recv()
                    total = total + rb[a % NZ].astype(F32)
        return total

    for a, b in REDUCE[0]:
        pull(a % NZ, 0)
        sb[a % NZ] = own[a % NZ].astype(BF16)
        back(a, b).start()
    for edges in REDUCE[1:]:
        for a, b in edges:
            pull(a % NZ, 0)
    pull(0, 0)
    for edges in REDUCE[1:]:
        for a, b in edges:
            sb[a % NZ] = summed(a).astype(BF16)
            back(a, b).start()

    def w_sum(i, total):
        w_ring(i).wait_recv()
        return total

    lax.fori_loop(0, NZ - 1, w_sum, 0)
    piece = dwz[0].astype(F32)
    for t in range(1, NZ):
        piece = piece + dwz[t].astype(F32)
    dwf[core, CHIPS] = piece[8:16]
    dwf[core, me] = piece[0:8]

    def w_gather(i, src):
        return remote(
            dwf.at[core, src], dwf.at[core, src], was.at[i], war.at[i], at_chip(i)
        )

    def w_gather_start(i, carry):
        w_gather(i, me).start()
        return carry

    lax.fori_loop(0, CHIPS - 1, w_gather_start, 0)

    total = summed(0)
    df_v[...] = total.T.astype(BF16)
    st_df = pltpu.make_async_copy(df_v, df_out, lsem.at[6])
    st_df.start()

    def w_gather_wait(i, carry):
        w_gather(i, chip(i, -1)).wait_recv()
        return carry

    lax.fori_loop(0, CHIPS - 1, w_gather_wait, 0)
    w_back = remote(dwf.at[core], dwf.at[core], ws.at[1], wr.at[1], twin)
    w_back.start()

    w_in = remote(dwf.at[other], dwf.at[other], ws.at[1], wr.at[1], twin)
    w_in.wait_recv()
    for half in range(2):
        lanes = slice(half * 128, half * 128 + 128)
        dwo[:, lanes] = dwf[half, 0:CHIPS].reshape(F_IN, 128)
        dbo[:, lanes] = dwf[half, CHIPS, 0:1]
    st_dw = pltpu.make_async_copy(dwo, dw_out, lsem.at[7])
    st_dw.start()
    st_db = pltpu.make_async_copy(dbo, db_out, lsem.at[8])
    st_db.start()

    def drain(i, carry):
        remote(sd.at[i], rd.at[i], ds.at[i], dr.at[i], twin).wait_send()
        remote(ga.at[c], ga.at[c], gs.at[i], gr.at[i], twin).wait_send()
        return carry

    lax.fori_loop(0, CHIPS, drain, 0)

    def drain_15(i, carry):
        remote(sz.at[i], rz.at[i], xs.at[i], xr.at[i], twin).wait_send()
        remote(ga.at[c], ga.at[c], fs.at[i], fr.at[i], twin).wait_send()
        remote(dwm.at[0], dwx.at[i], wxs.at[i], wxr.at[i], twin).wait_send()
        remote(dwz.at[z], dwz.at[z], wzs.at[i], wzr.at[i], twin).wait_send()
        w_gather(i, me).wait_send()
        remote(xa.at[z], xa.at[z], zs.at[i + 1], zr.at[i + 1], twin).wait_send()
        remote(sb.at[i], rb.at[i], bs.at[i + 1], br.at[i + 1], twin).wait_send()
        return carry

    lax.fori_loop(0, CHIPS - 1, drain_15, 0)
    w_twin.wait_send()
    w_back.wait_send()
    for st in (st_act, st_df, st_dw, st_db):
        st.wait()


def hand_over(*refs):
    n = len(refs) // 2
    sem = refs[-1]
    moves = [
        pltpu.make_async_copy(refs[i], refs[n + i], sem.at[i]) for i in range(n)
    ]
    for move in moves:
        move.start()
    for move in moves:
        move.wait()


def local(features, weight, bias, adj_values, adj_rows, cotangent):
    any_space = pl.BlockSpec(memory_space=pl.ANY)
    dma = pltpu.SemaphoreType.DMA
    outs = pl.pallas_call(
        kernel,
        out_shape=(
            jax.ShapeDtypeStruct((BLOCK, F_OUT), BF16),
            jax.ShapeDtypeStruct((BLOCK, F_IN), BF16),
            jax.ShapeDtypeStruct((F_IN, F_OUT), F32),
            jax.ShapeDtypeStruct((1, F_OUT), F32),
        ),
        in_specs=[pl.BlockSpec(memory_space=pltpu.SMEM)] + [any_space] * 5,
        out_specs=[any_space] * 4,
        scratch_shapes=[
            pltpu.VMEM((NZ, BLOCK, F_IN), BF16),
            pltpu.VMEM((DEAD, BLOCK, BLOCK), BF16),
            pltpu.VMEM((DEAD + 1, BLOCK, F_IN), F32),
            pltpu.SMEM((NZ, NCOL), jnp.int32),
            pltpu.VMEM((F_IN, F_OUT), BF16),
            pltpu.VMEM((1, F_OUT), F32),
            pltpu.VMEM((BLOCK, F_OUT), BF16),
            pltpu.VMEM((BLOCK, F_OUT), BF16),
            pltpu.VMEM((CHIPS, BLOCK, F_IN), BF16),
            pltpu.VMEM((CHIPS, BLOCK, F_IN), BF16),
            pltpu.VMEM((CHIPS - 1, BLOCK, F_IN), BF16),
            pltpu.VMEM((CHIPS - 1, BLOCK, F_IN), BF16),
            pltpu.VMEM((NCOL + 1, F_IN, BLOCK), BF16),
            pltpu.VMEM((NZ, F_IN, BLOCK), F32),
            pltpu.VMEM((NZ, F_IN, BLOCK), BF16),
            pltpu.VMEM((NZ, F_IN, BLOCK), BF16),
            pltpu.VMEM((BLOCK, F_IN), BF16),
            pltpu.VMEM((CHIPS, 16, F_OUT), BF16),
            pltpu.VMEM((CHIPS - 1, 16, F_OUT), BF16),
            pltpu.VMEM((2, 16, 128), F32),
            pltpu.VMEM((NZ, 16, 128), BF16),
            pltpu.VMEM((2, CHIPS + 1, 8, 128), F32),
            pltpu.VMEM((F_IN, F_OUT), F32),
            pltpu.VMEM((1, F_OUT), F32),
            dma((9,)),
            dma((16,)),
            dma((16,)), dma((16,)),
            dma((16,)), dma((16,)),
            dma((15,)), dma((15,)),
            dma((16,)), dma((16,)),
            dma((15,)), dma((15,)),
            dma((16,)), dma((16,)),
            dma((2,)), dma((2,)),
            dma((15,)), dma((15,)),
            dma((15,)), dma((15,)),
            dma((15,)), dma((15,)),
        ],
        compiler_params=pltpu.CompilerParams(
            collective_id=0, has_side_effects=True, vmem_limit_bytes=56 << 20
        ),
    )(
        jnp.transpose(adj_rows, (2, 0, 1)),
        features,
        weight,
        bias.reshape(1, F_OUT),
        adj_values.reshape(DEAD, BLOCK, BLOCK),
        cotangent,
    )
    activations, dfeatures, dweight, dbias = pl.pallas_call(
        hand_over,
        out_shape=tuple(jax.ShapeDtypeStruct(o.shape, o.dtype) for o in outs),
        in_specs=[pl.BlockSpec(memory_space=pltpu.VMEM)] * 4,
        out_specs=[any_space] * 4,
        scratch_shapes=[dma((4,))],
    )(*outs)
    return activations, dfeatures, dweight, dbias.reshape(F_OUT)


def solution(mesh):
    return jax.shard_map(
        local,
        mesh=mesh,
        in_specs=(
            P(("row", "col"), None),
            P(),
            P(),
            P("row", "col", None, None, None),
            P("row", "col", None),
            P(("row", "col"), None),
        ),
        out_specs=(P(("row", "col"), None), P(("row", "col"), None), P(), P()),
        check_vma=False,
    )
```

```python
import jax
import jax.numpy as jnp
from jax import lax
from jax.experimental import pallas as pl
from jax.experimental.pallas import tpu as pltpu
from jax.sharding import PartitionSpec as P

MESH = pl.DeviceIdType.MESH
BF16 = jnp.bfloat16
F32 = jnp.float32
BLOCK = 128
F_IN = 128
F_OUT = 256
SLOTS = 6
NZ = 16
SIDE = 4
CHIPS = SIDE * SIDE
NCOL = 2 * CHIPS
DEAD = NZ * SLOTS
LAG = 2
HALFWAY = 0
GATHER = (
    ((0, 3), (0, -3), (0, 1), (0, -1)),
    ((3, 6), (-3, -6), (1, 2), (-1, -2), (3, 4), (-3, -4)),
    ((6, 8), (6, 7), (-6, -7), (6, 5), (-6, -5)),
)
REDUCE = (
    ((8, 6), (7, 6), (-7, -6), (5, 6), (-5, -6), (4, 3), (-4, -3), (1, 0), (-1, 0)),
    ((6, 3), (-6, -3), (2, 0), (-2, 0)),
    ((3, 0), (-3, 0)),
)


def remote(src, dst, send_sem, recv_sem, device):
    return pltpu.make_async_remote_copy(
        src_ref=src,
        dst_ref=dst,
        send_sem=send_sem,
        recv_sem=recv_sem,
        device_id=device,
        device_id_type=MESH,
    )


def kernel(
    ids, feat, weight, bias, vals, cot,
    act_out, df_out, dw_out, db_out,
    adj, xa, blk, prod, inv, w_v, b_v, c_v, act_v,
    sd, rd, sz, rz, ga, own, sb, rb, df_v,
    dwm, dwx, dwt, dwz, dwf, dwo, dbo,
    lsem, asem, zs, zr, ds, dr, xs, xr, gs, gr, fs, fr, bs, br, ws, wr,
    wxs, wxr, wzs, wzr, was, war,
):
    z = lax.axis_index("row")
    c = lax.axis_index("col")
    px, py, core = c // 8, (c // 2) % 4, c % 2
    other = 1 - core

    def ring(off):
        return lax.rem(z + (off + 2 * NZ), NZ)

    def at_z(off):
        return (ring(off), c)

    def far_first(a):
        return jnp.where(a == 0, 2, jnp.where(a == 1, 1, jnp.where(a == 2, 3, 0)))

    def chip(i, sign):
        dx, dy = far_first(i // SIDE), far_first(lax.rem(i, SIDE))
        qx = lax.rem(px + SIDE + sign * dx, SIDE)
        qy = lax.rem(py + SIDE + sign * dy, SIDE)
        return qx * SIDE + qy

    def at_chip(i):
        return (z, 2 * chip(i, 1) + core)

    twin = (z, 2 * (px * SIDE + py) + other)

    ld_x = pltpu.make_async_copy(feat, xa.at[z], lsem.at[0])
    ld_i = pltpu.make_async_copy(ids, adj, lsem.at[1])
    ld_w = pltpu.make_async_copy(weight, w_v, lsem.at[2])
    ld_b = pltpu.make_async_copy(bias, b_v, lsem.at[3])
    ld_c = pltpu.make_async_copy(cot, c_v, lsem.at[4])

    def ld_a(t):
        part = pl.ds(t * SLOTS, SLOTS)
        return pltpu.make_async_copy(vals.at[part], blk.at[part], asem.at[t])

    def ld_a_start(t, carry):
        ld_a(t).start()
        return carry

    barrier = pltpu.get_barrier_semaphore()
    for off in (3, -3, 1, -1):
        pl.semaphore_signal(barrier, inc=1, device_id=at_z(off), device_id_type=MESH)
    ld_x.start()
    ld_i.start()

    def greet(i, carry):
        pl.semaphore_signal(barrier, inc=1, device_id=at_chip(i), device_id_type=MESH)
        return carry

    lax.fori_loop(0, CHIPS - 1, greet, 0)
    pl.semaphore_signal(barrier, inc=1, device_id=twin, device_id_type=MESH)

    prod[DEAD] = jnp.zeros((BLOCK, F_IN), F32)
    ga[NCOL] = jnp.zeros((F_IN, BLOCK), BF16)
    ld_x.wait()
    pl.semaphore_wait(barrier, 4 + 1 + CHIPS - 1)

    def invert(t, carry):
        held = [adj[s, 0, t] for s in range(SLOTS)]
        for k in range(NCOL):
            slot = jnp.int32(DEAD)
            for s in range(SLOTS):
                slot = jnp.where(held[s] == k, t * SLOTS + s, slot)
            inv[t, k] = slot
        return carry

    def multiply(t):
        ld_a(t).wait()
        tall = blk[pl.ds(t * SLOTS, SLOTS)].reshape(SLOTS * BLOCK, BLOCK)
        out = jnp.dot(tall, xa[t], preferred_element_type=F32)
        prod[pl.ds(t * SLOTS, SLOTS)] = out.reshape(SLOTS, BLOCK, F_IN)

    def hop(a, b):
        block = xa.at[ring(-a)]
        return remote(block, block, zs.at[b % NZ], zr.at[b % NZ], at_z(b - a))

    here = {0}

    def arrive(b):
        if b not in here:
            hop(0, b).wait_recv()
            here.add(b)

    for stage, edges in enumerate(GATHER):
        for a, b in edges:
            arrive(a)
            hop(a, b).start()
        if stage == 0:
            lax.fori_loop(0, NZ, ld_a_start, 0)
            for ld in (ld_w, ld_b, ld_c):
                ld.start()
        if stage == 0:
            ld_i.wait()
        if stage < 2:
            lax.fori_loop(8 * stage, 8 * stage + 8, invert, 0)
        if stage == 1:
            for b in (0, 1, -1, 3, -3):
                multiply(ring(-b))
        if stage == 2:
            for b in (6, -6, 2, -2, 4, -4, 5, -5, 7, -7, 8):
                arrive(b)
                multiply(ring(-b))

    def placed(k):
        total = prod[inv[0, k]]
        for t in range(1, NZ):
            total = total + prod[inv[t, k]]
        return total

    def to_twin(i, carry):
        sd[i] = placed(2 * chip(i, 1) + other).astype(BF16)
        remote(sd.at[i], rd.at[i], ds.at[i], dr.at[i], twin).start()
        return carry

    def both(i):
        mine = placed(2 * chip(i, 1) + core)
        remote(sd.at[i], rd.at[i], ds.at[i], dr.at[i], twin).wait_recv()
        return mine + rd[i].astype(F32)

    def to_owner(i, carry):
        sz[i] = both(i).astype(BF16)
        remote(sz.at[i], rz.at[i], xs.at[i], xr.at[i], at_chip(i)).start()
        return carry

    lag = jnp.where(core == 1, CHIPS, LAG)

    def to_both(i, carry):
        to_twin(i, carry)
        return to_owner(i - lag, carry)

    lax.fori_loop(0, lag, to_twin, 0)
    lax.fori_loop(lag, CHIPS, to_both, 0)
    lax.fori_loop(CHIPS - lag, CHIPS - 1, to_owner, 0)
    own[0] = both(CHIPS - 1)

    def sent_x(i, carry):
        remote(xa.at[z], xa.at[z], zs.at[i], zr.at[i], twin).wait_send()
        return carry

    lax.fori_loop(1, NZ, sent_x, 0)

    def collect(i, carry):
        remote(sz.at[i], rz.at[i], xs.at[i], xr.at[i], at_chip(i)).wait_recv()
        own[0] += rz[i].astype(F32)
        return carry

    lax.fori_loop(0, CHIPS - 1, collect, 0)

    ld_w.wait()
    ld_b.wait()
    ld_c.wait()
    agg = own[0]
    agg_hi = agg.astype(BF16)
    agg_lo = (agg - agg_hi.astype(F32)).astype(BF16)
    w = w_v[...]
    hidden = jnp.dot(agg_hi, w, preferred_element_type=F32)
    hidden = hidden + jnp.dot(agg_lo, w, preferred_element_type=F32)
    preact = hidden + b_v[...]
    gate = jax.nn.sigmoid(preact)
    act_v[...] = (preact * gate).astype(BF16)
    st_act = pltpu.make_async_copy(act_v, act_out, lsem.at[5])
    st_act.start()
    dpre = c_v[...].astype(F32) * gate * (1.0 + preact * (1.0 - gate))
    dpre_round = dpre.astype(BF16)
    tn = (((0,), (0,)), ((), ()))
    dw = lax.dot_general(agg_hi, dpre_round, tn, preferred_element_type=F32)
    dw = dw + lax.dot_general(agg_lo, dpre_round, tn, preferred_element_type=F32)
    db = jnp.sum(dpre, axis=0, keepdims=True)
    first = lax.broadcasted_iota(jnp.int32, (8, F_OUT), 0) == 0
    db8 = jnp.where(first, jnp.broadcast_to(db, (8, F_OUT)), 0.0)
    for p in range(CHIPS):
        both_parts = jnp.concatenate([dw[8 * p : 8 * p + 8], db8], axis=0)
        dwm[p] = both_parts.astype(BF16)

    def w_spread(i, carry):
        remote(dwm.at[chip(i, 1)], dwx.at[i], wxs.at[i], wxr.at[i], at_chip(i)).start()
        return carry

    lax.fori_loop(0, CHIPS - 1, w_spread, 0)

    ga[c] = lax.dot_general(
        w, dpre_round, (((1,), (1,)), ((), ())), preferred_element_type=F32
    ).astype(BF16)

    def spread(i, carry):
        remote(ga.at[c], ga.at[c], gs.at[i], gr.at[i], at_chip(i)).start()
        return carry

    lax.fori_loop(0, CHIPS - 1, spread, 0)
    g_twin = remote(ga.at[c], ga.at[c], gs.at[CHIPS - 1], gr.at[CHIPS - 1], twin)
    g_twin.start()

    def sent_sums(i, carry):
        remote(sd.at[i], rd.at[i], ds.at[i], dr.at[i], twin).wait_send()
        remote(sz.at[i], rz.at[i], xs.at[i], xr.at[i], twin).wait_send()
        return carry

    lax.fori_loop(0, CHIPS - 1, sent_sums, 0)
    last = CHIPS - 1
    remote(sd.at[last], rd.at[last], ds.at[last], dr.at[last], twin).wait_send()

    def w_collect(i, total):
        remote(dwm.at[0], dwx.at[i], wxs.at[i], wxr.at[i], at_chip(i)).wait_recv()
        return total + dwx[i].astype(F32)

    me = px * SIDE + py
    mixed = lax.fori_loop(0, CHIPS - 1, w_collect, dwm[me].astype(F32))
    left, right = mixed[:, 0:128], mixed[:, 128:F_OUT]
    dwt[0] = jnp.where(core == 0, right, left)
    w_twin = remote(dwt.at[0], dwt.at[1], ws.at[0], wr.at[0], twin)
    w_twin.start()

    def forward(i, carry):
        src = 2 * chip(i, -1) + core
        remote(ga.at[src], ga.at[src], gs.at[i], gr.at[i], at_chip(i)).wait_recv()
        remote(ga.at[src], ga.at[src], fs.at[i], fr.at[i], twin).start()
        return carry

    lax.fori_loop(0, HALFWAY, forward, 0)
    w_twin.wait_recv()
    dwz[z] = (jnp.where(core == 0, left, right) + dwt[1]).astype(BF16)

    def w_ring(i):
        step = (i + 1) // 2
        off = jnp.where(lax.rem(i, 2) == 0, 8 + step, 8 - step)
        return remote(dwz.at[z], dwz.at[z], wzs.at[i], wzr.at[i], at_z(off))

    def w_ring_start(i, carry):
        w_ring(i).start()
        return carry

    lax.fori_loop(0, NZ - 1, w_ring_start, 0)
    lax.fori_loop(HALFWAY, CHIPS - 1, forward, 0)

    g_twin.wait_recv()

    def from_twin(i, carry):
        src = 2 * chip(i, -1) + other
        remote(ga.at[src], ga.at[src], fs.at[i], fr.at[i], twin).wait_recv()
        return carry

    lax.fori_loop(0, CHIPS - 1, from_twin, 0)

    def pull(i, carry):
        t = ring(-i)
        picks = []
        for s in range(SLOTS):
            k = adj[s, 0, t]
            picks.append(ga[jnp.where(k < 0, NCOL, k)])
        wide = jnp.concatenate(picks, axis=1)
        tall = blk[pl.ds(t * SLOTS, SLOTS)].reshape(SLOTS * BLOCK, BLOCK)
        own[i] = jnp.dot(wide, tall, preferred_element_type=F32)
        return carry

    def back(a, b):
        n = a % NZ
        return remote(sb.at[n], rb.at[n], bs.at[n], br.at[n], at_z(b - a))

    def summed(b):
        total = own[b % NZ]
        for edges in REDUCE:
            for a, to in edges:
                if to == b:
                    back(a, b).wait_recv()
                    total = total + rb[a % NZ].astype(F32)
        return total

    for a, b in REDUCE[0]:
        pull(a % NZ, 0)
        sb[a % NZ] = own[a % NZ].astype(BF16)
        back(a, b).start()
    for edges in REDUCE[1:]:
        for a, b in edges:
            pull(a % NZ, 0)
    pull(0, 0)

    def sent_grads(i, carry):
        remote(ga.at[c], ga.at[c], gs.at[i], gr.at[i], twin).wait_send()
        remote(ga.at[c], ga.at[c], fs.at[i], fr.at[i], twin).wait_send()
        remote(dwm.at[0], dwx.at[i], wxs.at[i], wxr.at[i], twin).wait_send()
        return carry

    lax.fori_loop(0, CHIPS - 1, sent_grads, 0)
    g_twin.wait_send()
    w_twin.wait_send()
    for edges in REDUCE[1:-1]:
        for a, b in edges:
            sb[a % NZ] = summed(a).astype(BF16)
            back(a, b).start()

    def w_sum(i, total):
        w_ring(i).wait_recv()
        return total

    lax.fori_loop(0, NZ - 1, w_sum, 0)
    piece = dwz[0].astype(F32)
    for t in range(1, NZ):
        piece = piece + dwz[t].astype(F32)
    dwf[core, CHIPS] = piece[8:16]
    dwf[core, me] = piece[0:8]

    def w_gather(i, src):
        return remote(
            dwf.at[core, src], dwf.at[core, src], was.at[i], war.at[i], at_chip(i)
        )

    def w_gather_start(i, carry):
        w_gather(i, me).start()
        return carry

    lax.fori_loop(0, CHIPS - 1, w_gather_start, 0)

    for a, b in REDUCE[-1]:
        sb[a % NZ] = summed(a).astype(BF16)
        back(a, b).start()

    for a, b in REDUCE[0]:
        back(a, b).wait_send()

    def w_gather_wait(i, carry):
        w_gather(i, chip(i, -1)).wait_recv()
        return carry

    lax.fori_loop(0, CHIPS - 1, w_gather_wait, 0)
    w_back = remote(dwf.at[core], dwf.at[core], ws.at[1], wr.at[1], twin)
    w_back.start()

    def sent_pieces(i, carry):
        w_ring(i).wait_send()
        w_gather(i, me).wait_send()
        return carry

    lax.fori_loop(0, CHIPS - 1, sent_pieces, 0)

    total = summed(0)
    df_v[...] = total.T.astype(BF16)
    st_df = pltpu.make_async_copy(df_v, df_out, lsem.at[6])
    st_df.start()

    w_in = remote(dwf.at[other], dwf.at[other], ws.at[1], wr.at[1], twin)
    w_in.wait_recv()
    for half in range(2):
        lanes = slice(half * 128, half * 128 + 128)
        dwo[:, lanes] = dwf[half, 0:CHIPS].reshape(F_IN, 128)
        dbo[:, lanes] = dwf[half, CHIPS, 0:1]
    st_dw = pltpu.make_async_copy(dwo, dw_out, lsem.at[7])
    st_dw.start()
    st_db = pltpu.make_async_copy(dbo, db_out, lsem.at[8])
    st_db.start()

    for edges in REDUCE[1:]:
        for a, b in edges:
            back(a, b).wait_send()
    w_back.wait_send()
    for st in (st_act, st_df, st_dw, st_db):
        st.wait()


def hand_over(*refs):
    n = len(refs) // 2
    sem = refs[-1]
    moves = [
        pltpu.make_async_copy(refs[i], refs[n + i], sem.at[i]) for i in range(n)
    ]
    for move in moves:
        move.start()
    for move in moves:
        move.wait()


def local(features, weight, bias, adj_values, adj_rows, cotangent):
    any_space = pl.BlockSpec(memory_space=pl.ANY)
    dma = pltpu.SemaphoreType.DMA
    outs = pl.pallas_call(
        kernel,
        out_shape=(
            jax.ShapeDtypeStruct((BLOCK, F_OUT), BF16),
            jax.ShapeDtypeStruct((BLOCK, F_IN), BF16),
            jax.ShapeDtypeStruct((F_IN, F_OUT), F32),
            jax.ShapeDtypeStruct((1, F_OUT), F32),
        ),
        in_specs=[any_space] * 6,
        out_specs=[any_space] * 4,
        scratch_shapes=[
            pltpu.SMEM((SLOTS, 1, NZ), jnp.int32),
            pltpu.VMEM((NZ, BLOCK, F_IN), BF16),
            pltpu.VMEM((DEAD, BLOCK, BLOCK), BF16),
            pltpu.VMEM((DEAD + 1, BLOCK, F_IN), F32),
            pltpu.SMEM((NZ, NCOL), jnp.int32),
            pltpu.VMEM((F_IN, F_OUT), BF16),
            pltpu.VMEM((1, F_OUT), F32),
            pltpu.VMEM((BLOCK, F_OUT), BF16),
            pltpu.VMEM((BLOCK, F_OUT), BF16),
            pltpu.VMEM((CHIPS, BLOCK, F_IN), BF16),
            pltpu.VMEM((CHIPS, BLOCK, F_IN), BF16),
            pltpu.VMEM((CHIPS - 1, BLOCK, F_IN), BF16),
            pltpu.VMEM((CHIPS - 1, BLOCK, F_IN), BF16),
            pltpu.VMEM((NCOL + 1, F_IN, BLOCK), BF16),
            pltpu.VMEM((NZ, F_IN, BLOCK), F32),
            pltpu.VMEM((NZ, F_IN, BLOCK), BF16),
            pltpu.VMEM((NZ, F_IN, BLOCK), BF16),
            pltpu.VMEM((BLOCK, F_IN), BF16),
            pltpu.VMEM((CHIPS, 16, F_OUT), BF16),
            pltpu.VMEM((CHIPS - 1, 16, F_OUT), BF16),
            pltpu.VMEM((2, 16, 128), F32),
            pltpu.VMEM((NZ, 16, 128), BF16),
            pltpu.VMEM((2, CHIPS + 1, 8, 128), F32),
            pltpu.VMEM((F_IN, F_OUT), F32),
            pltpu.VMEM((1, F_OUT), F32),
            dma((9,)),
            dma((16,)),
            dma((16,)), dma((16,)),
            dma((16,)), dma((16,)),
            dma((15,)), dma((15,)),
            dma((16,)), dma((16,)),
            dma((15,)), dma((15,)),
            dma((16,)), dma((16,)),
            dma((2,)), dma((2,)),
            dma((15,)), dma((15,)),
            dma((15,)), dma((15,)),
            dma((15,)), dma((15,)),
        ],
        compiler_params=pltpu.CompilerParams(
            collective_id=0, has_side_effects=True, vmem_limit_bytes=56 << 20
        ),
    )(
        jnp.transpose(adj_rows, (2, 0, 1)),
        features,
        weight,
        bias.reshape(1, F_OUT),
        adj_values.reshape(DEAD, BLOCK, BLOCK),
        cotangent,
    )
    activations, dfeatures, dweight, dbias = pl.pallas_call(
        hand_over,
        out_shape=tuple(jax.ShapeDtypeStruct(o.shape, o.dtype) for o in outs),
        in_specs=[pl.BlockSpec(memory_space=pltpu.VMEM)] * 4,
        out_specs=[any_space] * 4,
        scratch_shapes=[dma((4,))],
    )(*outs)
    return activations, dfeatures, dweight, dbias.reshape(F_OUT)


def solution(mesh):
    return jax.shard_map(
        local,
        mesh=mesh,
        in_specs=(
            P(("row", "col"), None),
            P(),
            P(),
            P("row", "col", None, None, None),
            P("row", "col", None),
            P(("row", "col"), None),
        ),
        out_specs=(P(("row", "col"), None), P(("row", "col"), None), P(), P()),
        check_vma=False,
    )
```

```python
import jax
import jax.numpy as jnp
from jax import lax
from jax.experimental import pallas as pl
from jax.experimental.pallas import tpu as pltpu
from jax.sharding import PartitionSpec as P

MESH = pl.DeviceIdType.MESH
BF16 = jnp.bfloat16
F32 = jnp.float32
BLOCK = 128
F_IN = 128
F_OUT = 256
SLOTS = 6
NZ = 16
SIDE = 4
CHIPS = SIDE * SIDE
NCOL = 2 * CHIPS
DEAD = NZ * SLOTS
LAG = 2
EARLY = (4, 8, 12, 16)
HALFWAY = 0
GATHER = (
    ((0, 3), (0, -3), (0, 1), (0, -1)),
    ((3, 6), (-3, -6), (1, 2), (-1, -2), (3, 4), (-3, -4)),
    ((6, 8), (6, 7), (-6, -7), (6, 5), (-6, -5)),
)
REDUCE = (
    ((8, 6), (7, 6), (-7, -6), (5, 6), (-5, -6), (4, 3), (-4, -3), (1, 0), (-1, 0), (2, 0), (-2, 0)),
    ((6, 3), (-6, -3)),
    ((3, 0), (-3, 0)),
)


def remote(src, dst, send_sem, recv_sem, device):
    return pltpu.make_async_remote_copy(
        src_ref=src,
        dst_ref=dst,
        send_sem=send_sem,
        recv_sem=recv_sem,
        device_id=device,
        device_id_type=MESH,
    )


def kernel(
    ids, feat, weight, bias, vals, cot,
    act_out, df_out, dw_out, db_out,
    adj, xa, blk, prod, inv, w_v, b_v, c_v, act_v,
    sd, rd, sz, rz, ga, own, sb, rb, df_v,
    dwm, dwx, dwt, dwz, dwf, dwo, dbo,
    lsem, asem, zs, zr, ds, dr, xs, xr, gs, gr, fs, fr, bs, br, ws, wr,
    wxs, wxr, wzs, wzr, was, war,
):
    z = lax.axis_index("row")
    c = lax.axis_index("col")
    px, py, core = c // 8, (c // 2) % 4, c % 2
    other = 1 - core

    def ring(off):
        return lax.rem(z + (off + 2 * NZ), NZ)

    def at_z(off):
        return (ring(off), c)

    def far_first(a):
        return jnp.where(a == 0, 2, jnp.where(a == 1, 1, jnp.where(a == 2, 3, 0)))

    def chip(i, sign):
        dx, dy = far_first(i // SIDE), far_first(lax.rem(i, SIDE))
        qx = lax.rem(px + SIDE + sign * dx, SIDE)
        qy = lax.rem(py + SIDE + sign * dy, SIDE)
        return qx * SIDE + qy

    def at_chip(i):
        return (z, 2 * chip(i, 1) + core)

    twin = (z, 2 * (px * SIDE + py) + other)

    ld_x = pltpu.make_async_copy(feat, xa.at[z], lsem.at[0])
    ld_i = pltpu.make_async_copy(ids, adj, lsem.at[1])
    ld_w = pltpu.make_async_copy(weight, w_v, lsem.at[2])
    ld_b = pltpu.make_async_copy(bias, b_v, lsem.at[3])
    ld_c = pltpu.make_async_copy(cot, c_v, lsem.at[4])

    def ld_a(t):
        part = pl.ds(t * SLOTS, SLOTS)
        return pltpu.make_async_copy(vals.at[part], blk.at[part], asem.at[t])

    def ld_a_start(t, carry):
        ld_a(t).start()
        return carry

    barrier = pltpu.get_barrier_semaphore()
    for off in (3, -3, 1, -1):
        pl.semaphore_signal(barrier, inc=1, device_id=at_z(off), device_id_type=MESH)
    ld_x.start()
    ld_i.start()

    def greet(i, carry):
        pl.semaphore_signal(barrier, inc=1, device_id=at_chip(i), device_id_type=MESH)
        return carry

    lax.fori_loop(0, CHIPS - 1, greet, 0)
    pl.semaphore_signal(barrier, inc=1, device_id=twin, device_id_type=MESH)

    prod[DEAD] = jnp.zeros((BLOCK, F_IN), F32)
    ga[NCOL] = jnp.zeros((F_IN, BLOCK), BF16)
    lax.fori_loop(0, NZ, ld_a_start, 0)
    for ld in (ld_w, ld_b, ld_c):
        ld.start()

    def invert(t, carry):
        held = [adj[s, 0, t] for s in range(SLOTS)]
        for k in range(NCOL):
            slot = jnp.int32(DEAD)
            for s in range(SLOTS):
                slot = jnp.where(held[s] == k, t * SLOTS + s, slot)
            inv[t, k] = slot
        return carry

    ld_i.wait()
    lax.fori_loop(0, EARLY[0], invert, 0)
    ld_x.wait()
    pl.semaphore_wait(barrier, 4 + 1 + CHIPS - 1)


    def multiply(t):
        ld_a(t).wait()
        tall = blk[pl.ds(t * SLOTS, SLOTS)].reshape(SLOTS * BLOCK, BLOCK)
        out = jnp.dot(tall, xa[t], preferred_element_type=F32)
        prod[pl.ds(t * SLOTS, SLOTS)] = out.reshape(SLOTS, BLOCK, F_IN)

    def hop(a, b):
        block = xa.at[ring(-a)]
        return remote(block, block, zs.at[b % NZ], zr.at[b % NZ], at_z(b - a))

    here = {0}

    def arrive(b):
        if b not in here:
            hop(0, b).wait_recv()
            here.add(b)

    for stage, edges in enumerate(GATHER):
        for a, b in edges:
            arrive(a)
            hop(a, b).start()
        lax.fori_loop(EARLY[stage], EARLY[stage + 1], invert, 0)
        if stage == 1:
            for b in (0, 1, -1, 3, -3):
                multiply(ring(-b))
        if stage == 2:
            for b in (6, -6, 2, -2, 4, -4, 5, -5, 7, -7, 8):
                arrive(b)
                multiply(ring(-b))

    def placed(k):
        total = prod[inv[0, k]]
        for t in range(1, NZ):
            total = total + prod[inv[t, k]]
        return total

    def to_twin(i, carry):
        sd[i] = placed(2 * chip(i, 1) + other).astype(BF16)
        remote(sd.at[i], rd.at[i], ds.at[i], dr.at[i], twin).start()
        return carry

    def both(i):
        mine = placed(2 * chip(i, 1) + core)
        remote(sd.at[i], rd.at[i], ds.at[i], dr.at[i], twin).wait_recv()
        return mine + rd[i].astype(F32)

    def to_owner(i, carry):
        sz[i] = both(i).astype(BF16)
        remote(sz.at[i], rz.at[i], xs.at[i], xr.at[i], at_chip(i)).start()
        return carry

    lag = jnp.where(core == 1, CHIPS, LAG)

    def to_both(i, carry):
        to_twin(i, carry)
        return to_owner(i - lag, carry)

    lax.fori_loop(0, lag, to_twin, 0)
    lax.fori_loop(lag, CHIPS, to_both, 0)
    lax.fori_loop(CHIPS - lag, CHIPS - 1, to_owner, 0)
    own[0] = both(CHIPS - 1)

    def sent_x(i, carry):
        remote(xa.at[z], xa.at[z], zs.at[i], zr.at[i], twin).wait_send()
        return carry

    lax.fori_loop(1, NZ, sent_x, 0)

    def collect(i, carry):
        remote(sz.at[i], rz.at[i], xs.at[i], xr.at[i], at_chip(i)).wait_recv()
        own[0] += rz[i].astype(F32)
        return carry

    lax.fori_loop(0, CHIPS - 1, collect, 0)

    ld_w.wait()
    ld_b.wait()
    ld_c.wait()
    agg = own[0]
    agg_hi = agg.astype(BF16)
    agg_lo = (agg - agg_hi.astype(F32)).astype(BF16)
    w = w_v[...]
    hidden = jnp.dot(agg_hi, w, preferred_element_type=F32)
    hidden = hidden + jnp.dot(agg_lo, w, preferred_element_type=F32)
    preact = hidden + b_v[...]
    gate = jax.nn.sigmoid(preact)
    act_v[...] = (preact * gate).astype(BF16)
    st_act = pltpu.make_async_copy(act_v, act_out, lsem.at[5])
    st_act.start()
    dpre = c_v[...].astype(F32) * gate * (1.0 + preact * (1.0 - gate))
    dpre_round = dpre.astype(BF16)
    tn = (((0,), (0,)), ((), ()))
    dw = lax.dot_general(agg_hi, dpre_round, tn, preferred_element_type=F32)
    dw = dw + lax.dot_general(agg_lo, dpre_round, tn, preferred_element_type=F32)
    db = jnp.sum(dpre, axis=0, keepdims=True)
    first = lax.broadcasted_iota(jnp.int32, (8, F_OUT), 0) == 0
    db8 = jnp.where(first, jnp.broadcast_to(db, (8, F_OUT)), 0.0)
    for p in range(CHIPS):
        both_parts = jnp.concatenate([dw[8 * p : 8 * p + 8], db8], axis=0)
        dwm[p] = both_parts.astype(BF16)

    def w_spread(i, carry):
        remote(dwm.at[chip(i, 1)], dwx.at[i], wxs.at[i], wxr.at[i], at_chip(i)).start()
        return carry

    lax.fori_loop(0, CHIPS - 1, w_spread, 0)

    ga[c] = lax.dot_general(
        w, dpre_round, (((1,), (1,)), ((), ())), preferred_element_type=F32
    ).astype(BF16)

    def spread(i, carry):
        remote(ga.at[c], ga.at[c], gs.at[i], gr.at[i], at_chip(i)).start()
        return carry

    lax.fori_loop(0, CHIPS - 1, spread, 0)
    g_twin = remote(ga.at[c], ga.at[c], gs.at[CHIPS - 1], gr.at[CHIPS - 1], twin)
    g_twin.start()

    def sent_sums(i, carry):
        remote(sd.at[i], rd.at[i], ds.at[i], dr.at[i], twin).wait_send()
        remote(sz.at[i], rz.at[i], xs.at[i], xr.at[i], twin).wait_send()
        return carry

    lax.fori_loop(0, CHIPS - 1, sent_sums, 0)
    last = CHIPS - 1
    remote(sd.at[last], rd.at[last], ds.at[last], dr.at[last], twin).wait_send()

    def w_collect(i, total):
        remote(dwm.at[0], dwx.at[i], wxs.at[i], wxr.at[i], at_chip(i)).wait_recv()
        return total + dwx[i].astype(F32)

    me = px * SIDE + py
    mixed = lax.fori_loop(0, CHIPS - 1, w_collect, dwm[me].astype(F32))
    left, right = mixed[:, 0:128], mixed[:, 128:F_OUT]
    dwt[0] = jnp.where(core == 0, right, left)
    w_twin = remote(dwt.at[0], dwt.at[1], ws.at[0], wr.at[0], twin)
    w_twin.start()

    def forward(i, carry):
        src = 2 * chip(i, -1) + core
        remote(ga.at[src], ga.at[src], gs.at[i], gr.at[i], at_chip(i)).wait_recv()
        remote(ga.at[src], ga.at[src], fs.at[i], fr.at[i], twin).start()
        return carry

    lax.fori_loop(0, HALFWAY, forward, 0)
    w_twin.wait_recv()
    dwz[z] = (jnp.where(core == 0, left, right) + dwt[1]).astype(BF16)

    def w_ring(i):
        step = (i + 1) // 2
        off = jnp.where(lax.rem(i, 2) == 0, 8 + step, 8 - step)
        return remote(dwz.at[z], dwz.at[z], wzs.at[i], wzr.at[i], at_z(off))

    def w_ring_start(i, carry):
        w_ring(i).start()
        return carry

    lax.fori_loop(0, NZ - 1, w_ring_start, 0)
    lax.fori_loop(HALFWAY, CHIPS - 1, forward, 0)

    g_twin.wait_recv()

    def from_twin(i, carry):
        src = 2 * chip(i, -1) + other
        remote(ga.at[src], ga.at[src], fs.at[i], fr.at[i], twin).wait_recv()
        return carry

    lax.fori_loop(0, CHIPS - 1, from_twin, 0)

    def pull(i, carry):
        t = ring(-i)
        picks = []
        for s in range(SLOTS):
            k = adj[s, 0, t]
            picks.append(ga[jnp.where(k < 0, NCOL, k)])
        wide = jnp.concatenate(picks, axis=1)
        tall = blk[pl.ds(t * SLOTS, SLOTS)].reshape(SLOTS * BLOCK, BLOCK)
        own[i] = jnp.dot(wide, tall, preferred_element_type=F32)
        return carry

    def back(a, b):
        n = a % NZ
        return remote(sb.at[n], rb.at[n], bs.at[n], br.at[n], at_z(b - a))

    def summed(b):
        total = own[b % NZ]
        for edges in REDUCE:
            for a, to in edges:
                if to == b:
                    back(a, b).wait_recv()
                    total = total + rb[a % NZ].astype(F32)
        return total

    for a, b in REDUCE[0]:
        pull(a % NZ, 0)
        sb[a % NZ] = own[a % NZ].astype(BF16)
        back(a, b).start()
    for edges in REDUCE[1:]:
        for a, b in edges:
            pull(a % NZ, 0)
    pull(0, 0)

    def sent_grads(i, carry):
        remote(ga.at[c], ga.at[c], gs.at[i], gr.at[i], twin).wait_send()
        remote(ga.at[c], ga.at[c], fs.at[i], fr.at[i], twin).wait_send()
        remote(dwm.at[0], dwx.at[i], wxs.at[i], wxr.at[i], twin).wait_send()
        return carry

    lax.fori_loop(0, CHIPS - 1, sent_grads, 0)
    g_twin.wait_send()
    w_twin.wait_send()
    for edges in REDUCE[1:-1]:
        for a, b in edges:
            sb[a % NZ] = summed(a).astype(BF16)
            back(a, b).start()

    def w_sum(i, total):
        w_ring(i).wait_recv()
        return total

    lax.fori_loop(0, NZ - 1, w_sum, 0)
    piece = dwz[0].astype(F32)
    for t in range(1, NZ):
        piece = piece + dwz[t].astype(F32)
    dwf[core, CHIPS] = piece[8:16]
    dwf[core, me] = piece[0:8]

    def w_gather(i, src):
        return remote(
            dwf.at[core, src], dwf.at[core, src], was.at[i], war.at[i], at_chip(i)
        )

    def w_gather_start(i, carry):
        w_gather(i, me).start()
        return carry

    lax.fori_loop(0, CHIPS - 1, w_gather_start, 0)

    for a, b in REDUCE[-1]:
        sb[a % NZ] = summed(a).astype(BF16)
        back(a, b).start()

    for a, b in REDUCE[0]:
        back(a, b).wait_send()

    def w_gather_wait(i, carry):
        w_gather(i, chip(i, -1)).wait_recv()
        return carry

    lax.fori_loop(0, CHIPS - 1, w_gather_wait, 0)
    w_back = remote(dwf.at[core], dwf.at[core], ws.at[1], wr.at[1], twin)
    w_back.start()

    def sent_pieces(i, carry):
        w_ring(i).wait_send()
        w_gather(i, me).wait_send()
        return carry

    lax.fori_loop(0, CHIPS - 1, sent_pieces, 0)

    total = summed(0)
    df_v[...] = total.T.astype(BF16)
    st_df = pltpu.make_async_copy(df_v, df_out, lsem.at[6])
    st_df.start()

    w_in = remote(dwf.at[other], dwf.at[other], ws.at[1], wr.at[1], twin)
    w_in.wait_recv()
    for half in range(2):
        lanes = slice(half * 128, half * 128 + 128)
        dwo[:, lanes] = dwf[half, 0:CHIPS].reshape(F_IN, 128)
        dbo[:, lanes] = dwf[half, CHIPS, 0:1]
    st_dw = pltpu.make_async_copy(dwo, dw_out, lsem.at[7])
    st_dw.start()
    st_db = pltpu.make_async_copy(dbo, db_out, lsem.at[8])
    st_db.start()

    for edges in REDUCE[1:]:
        for a, b in edges:
            back(a, b).wait_send()
    w_back.wait_send()
    for st in (st_act, st_df, st_dw, st_db):
        st.wait()


def hand_over(*refs):
    n = len(refs) // 2
    sem = refs[-1]
    moves = [
        pltpu.make_async_copy(refs[i], refs[n + i], sem.at[i]) for i in range(n)
    ]
    for move in moves:
        move.start()
    for move in moves:
        move.wait()


def local(features, weight, bias, adj_values, adj_rows, cotangent):
    any_space = pl.BlockSpec(memory_space=pl.ANY)
    dma = pltpu.SemaphoreType.DMA
    outs = pl.pallas_call(
        kernel,
        out_shape=(
            jax.ShapeDtypeStruct((BLOCK, F_OUT), BF16),
            jax.ShapeDtypeStruct((BLOCK, F_IN), BF16),
            jax.ShapeDtypeStruct((F_IN, F_OUT), F32),
            jax.ShapeDtypeStruct((1, F_OUT), F32),
        ),
        in_specs=[any_space] * 6,
        out_specs=[any_space] * 4,
        scratch_shapes=[
            pltpu.SMEM((SLOTS, 1, NZ), jnp.int32),
            pltpu.VMEM((NZ, BLOCK, F_IN), BF16),
            pltpu.VMEM((DEAD, BLOCK, BLOCK), BF16),
            pltpu.VMEM((DEAD + 1, BLOCK, F_IN), F32),
            pltpu.SMEM((NZ, NCOL), jnp.int32),
            pltpu.VMEM((F_IN, F_OUT), BF16),
            pltpu.VMEM((1, F_OUT), F32),
            pltpu.VMEM((BLOCK, F_OUT), BF16),
            pltpu.VMEM((BLOCK, F_OUT), BF16),
            pltpu.VMEM((CHIPS, BLOCK, F_IN), BF16),
            pltpu.VMEM((CHIPS, BLOCK, F_IN), BF16),
            pltpu.VMEM((CHIPS - 1, BLOCK, F_IN), BF16),
            pltpu.VMEM((CHIPS - 1, BLOCK, F_IN), BF16),
            pltpu.VMEM((NCOL + 1, F_IN, BLOCK), BF16),
            pltpu.VMEM((NZ, F_IN, BLOCK), F32),
            pltpu.VMEM((NZ, F_IN, BLOCK), BF16),
            pltpu.VMEM((NZ, F_IN, BLOCK), BF16),
            pltpu.VMEM((BLOCK, F_IN), BF16),
            pltpu.VMEM((CHIPS, 16, F_OUT), BF16),
            pltpu.VMEM((CHIPS - 1, 16, F_OUT), BF16),
            pltpu.VMEM((2, 16, 128), F32),
            pltpu.VMEM((NZ, 16, 128), BF16),
            pltpu.VMEM((2, CHIPS + 1, 8, 128), F32),
            pltpu.VMEM((F_IN, F_OUT), F32),
            pltpu.VMEM((1, F_OUT), F32),
            dma((9,)),
            dma((16,)),
            dma((16,)), dma((16,)),
            dma((16,)), dma((16,)),
            dma((15,)), dma((15,)),
            dma((16,)), dma((16,)),
            dma((15,)), dma((15,)),
            dma((16,)), dma((16,)),
            dma((2,)), dma((2,)),
            dma((15,)), dma((15,)),
            dma((15,)), dma((15,)),
            dma((15,)), dma((15,)),
        ],
        compiler_params=pltpu.CompilerParams(
            collective_id=0, has_side_effects=True, vmem_limit_bytes=56 << 20
        ),
    )(
        jnp.transpose(adj_rows, (2, 0, 1)),
        features,
        weight,
        bias.reshape(1, F_OUT),
        adj_values.reshape(DEAD, BLOCK, BLOCK),
        cotangent,
    )
    activations, dfeatures, dweight, dbias = pl.pallas_call(
        hand_over,
        out_shape=tuple(jax.ShapeDtypeStruct(o.shape, o.dtype) for o in outs),
        in_specs=[pl.BlockSpec(memory_space=pltpu.VMEM)] * 4,
        out_specs=[any_space] * 4,
        scratch_shapes=[dma((4,))],
    )(*outs)
    return activations, dfeatures, dweight, dbias.reshape(F_OUT)


def solution(mesh):
    return jax.shard_map(
        local,
        mesh=mesh,
        in_specs=(
            P(("row", "col"), None),
            P(),
            P(),
            P("row", "col", None, None, None),
            P("row", "col", None),
            P(("row", "col"), None),
        ),
        out_specs=(P(("row", "col"), None), P(("row", "col"), None), P(), P()),
        check_vma=False,
    )
```
